32 devices in a mesh: leaf: 4 (over y, x), front: 8 (over z, core).
Axes of the slice: x: 2, y: 2, z: 4, core: 2. Of those that a mesh axis runs over, the one named last changes fastest.
Arguments:
- factored_panel: bfloat16 [4096, 1536], P(('leaf', 'front')), may hold values from -2.5 to 2.5
- front_tiles: float32 [256, 128, 128], P(('leaf', 'front')), may hold values from -6 to 6
- ancestor_tiles: float32 [256, 128, 128], P(('leaf', 'front')), may hold values from -6 to 6
- send_slots: int32 [32, 8], P(('leaf', 'front')), may hold values from -1 to 3, as said below
- extend_slots: int32 [32, 4], P(('leaf', 'front')), may hold values from 0 to 7
Outputs:
- assembled: float32 [256, 128, 128], P(('leaf', 'front'))
The draws below stay inside these ranges and needn't reach their ends.
Inputs may be any that keep to these rules, and one draw needn't show every extreme that they name: `send_slots`: A value of -1 marks a block row without a tile; any other value is d + p, a leaf group d and a position p, and the values other than -1 in one row are distinct. In every leaf group the row of front index 0 uses all 4 values.
All inputs are finite; a program needn't handle non-finite values.
Results may differ from the reference program's by a relative error of at most 0.0003.
Values may be sent and summed in bfloat16 or wider, within the bound.
A program may use at most 64 MiB of HBM per device.

```python
import jax
import jax.numpy as jnp
from jax import lax

B = 128
PIV = 1536
CAP = 1
ANC = 8
UB = 8
N_LEAF = 4
N_FRONT = 8


def draw_send_slots(key, part):
    key = jax.random.fold_in(key, 11)
    message_slots = N_LEAF * CAP
    row_total = N_LEAF * N_FRONT
    perm_keys = jax.random.split(jax.random.fold_in(key, 2), row_total)
    orders = jax.vmap(lambda single: jax.random.permutation(single, message_slots))(perm_keys)
    pick_keys = jax.random.split(jax.random.fold_in(key, 3), row_total)
    priority = jax.vmap(lambda single: jax.random.permutation(single, UB))(pick_keys).astype(jnp.int32)
    front_index = (jnp.arange(row_total, dtype=jnp.int32) % N_FRONT)[:, None]
    block_row = jnp.arange(UB, dtype=jnp.int32)[None, :]
    forced = (block_row == (front_index + N_FRONT - 1) % N_FRONT) | (block_row == (front_index + 1) % N_FRONT) | (block_row == (front_index + N_FRONT // 2) % N_FRONT)
    priority = jnp.where(forced, priority, priority + UB).astype(jnp.int32)
    order_rank = jnp.argsort(jnp.argsort(priority, axis=1), axis=1).astype(jnp.int32)
    counts = jax.random.randint(jax.random.fold_in(key, 4), (row_total, 1), 3, message_slots + 1)
    counts = jnp.where(front_index == 0, message_slots, counts).astype(jnp.int32)
    live = order_rank < counts
    ranks = jnp.cumsum(live.astype(jnp.int32), axis=1) - 1
    picked = jnp.take_along_axis(orders.astype(jnp.int32), jnp.clip(ranks, 0, message_slots - 1), axis=1)
    return jnp.where(live, picked, -1).astype(jnp.int32)


def plant(values, key, low, high):
    index_at = [jax.random.randint(jax.random.fold_in(key, axis), (), 0, length) for axis, length in enumerate(values.shape)]
    widest = values.shape.index(max(values.shape))
    neighbour = index_at[:widest] + [(index_at[widest] + 1) % values.shape[widest]] + index_at[widest + 1:]
    return values.at[tuple(index_at)].set(low).at[tuple(neighbour)].set(high)


def levels(key, extent, cuts, low, largest):
    factor_of, own = 1.0, jax.random.fold_in(key, 6)
    for dim, parts in cuts:
        steps = jnp.exp(jax.random.uniform(jax.random.fold_in(own, dim), (parts,), jnp.float32, low / len(cuts), largest / len(cuts)))
        factor_of = factor_of * jnp.repeat(steps, extent[dim] // parts).reshape([-1 if axis == dim else 1 for axis in range(len(extent))])
    return factor_of


def scatter_about(own_key, dims, spread, most, cuts=(), kind=jnp.bfloat16):
    level = levels(own_key, dims, cuts, -0.22, 0.18) if cuts else 1.0
    result = jax.random.normal(own_key, dims, jnp.float32) * spread * level
    return jnp.minimum(jnp.maximum(result, -most), most).astype(kind)


def setup_inputs(seed: int = 0) -> dict:
    key_of = jax.random.split(jax.random.key(seed), 6)
    factored_panel = scatter_about(key_of[0], (N_LEAF * N_FRONT * B, PIV), 0.16, 2.5, ((0, 32),))
    front_tiles = scatter_about(key_of[1], (N_LEAF * N_FRONT * UB, B, B), 1.0, 6.0, ((0, 32),), jnp.float32)
    ancestor_tiles = scatter_about(key_of[2], (N_LEAF * N_FRONT * ANC, B, B), 1.0, 6.0, ((0, 32),), jnp.float32)
    send_slots = draw_send_slots(jax.random.fold_in(key_of[5], 71), 0)
    extend_slots = plant(jax.random.randint(key_of[4], (N_LEAF * N_FRONT, N_LEAF * CAP), 0, ANC), jax.random.fold_in(key_of[4], 1), 0, ANC - 1).astype(jnp.int32)
    return {"factored_panel": factored_panel, "front_tiles": front_tiles, "ancestor_tiles": ancestor_tiles, "send_slots": send_slots, "extend_slots": extend_slots}


def reference(factored_panel, front_tiles, ancestor_tiles, send_slots, extend_slots):
    grouped_panel = factored_panel.reshape(N_LEAF, N_FRONT * B, PIV)
    grouped_tiles = front_tiles.reshape(N_LEAF, N_FRONT, UB, B, B)
    grouped_targets = send_slots.reshape(N_LEAF, N_FRONT, UB)
    extend_table = extend_slots.reshape(N_LEAF * N_FRONT, N_LEAF * CAP)
    total_rows = N_LEAF * N_FRONT * ANC
    front_index = jnp.arange(N_FRONT, dtype=jnp.int32)[:, None]

    def one_group(assembled, inputs):
        group, panel_rows, tiles, targets = inputs
        products = jnp.dot(panel_rows, panel_rows.T, preferred_element_type=jnp.float32)
        products = products.reshape(UB, B, N_FRONT, B).transpose(2, 0, 1, 3)
        schur_tiles = tiles - products
        clipped = jnp.maximum(targets, 0).astype(jnp.int32)
        leaf_to = clipped // CAP
        position = clipped % CAP
        receiver = (leaf_to * N_FRONT + front_index).astype(jnp.int32)
        slot_in = extend_table[receiver, (group * CAP + position).astype(jnp.int32)]
        flat_index = (receiver * ANC + slot_in).astype(jnp.int32)
        flat_index = jnp.where(targets >= 0, flat_index, total_rows).astype(jnp.int32)
        assembled = assembled.at[flat_index.reshape(-1)].add(schur_tiles.reshape(-1, B, B), mode="drop")
        return assembled, jnp.zeros((), jnp.float32)

    groups = jnp.arange(N_LEAF, dtype=jnp.int32)
    scanned = lax.scan(one_group, ancestor_tiles, (groups, grouped_panel, grouped_tiles, grouped_targets))
    return scanned[0]
```

```python
import functools

import jax
import jax.numpy as jnp
from jax import lax
from jax.experimental import pallas as pl
from jax.experimental.pallas import tpu as pltpu
from jax.sharding import PartitionSpec as P

MESH = pl.DeviceIdType.MESH
UP, DOWN, SIDE = 0, 1, 2


def kernel(nz, n_leaf, chunks, panel, front, ancestor, targets, extend, out,
           held, schur, message, received, send_sem, recv_sem, leaf_send, leaf_recv):
    leaf = lax.axis_index("leaf")
    f = lax.axis_index("front")
    z, c = f // 2, f % 2
    side = f + 1 - 2 * c
    below, above = z > 0, z < nz - 1
    rows = panel.shape[0] // chunks
    blocks = schur.shape[0]

    barrier = pltpu.get_barrier_semaphore()

    def greet(device):
        pl.semaphore_signal(barrier, inc=1, device_id=device, device_id_type=MESH)

    pl.when(below)(lambda: greet((leaf, f - 2)))
    pl.when(above)(lambda: greet((leaf, f + 2)))
    greet((leaf, side))
    for j in range(1, n_leaf):
        greet(((leaf + j) % n_leaf, f))
    pl.semaphore_wait(
        barrier, n_leaf + below.astype(jnp.int32) + above.astype(jnp.int32)
    )

    def piece(ref, k):
        return ref.at[pl.ds(k * rows, rows)]

    def copy(way, source, block, k):
        to = {UP: f + 2, DOWN: f - 2, SIDE: side}[way]
        return pltpu.make_async_remote_copy(
            src_ref=piece(source, k),
            dst_ref=piece(held.at[block], k),
            send_sem=send_sem.at[way, block, k],
            recv_sem=recv_sem.at[block, k],
            device_id=(leaf, to),
            device_id_type=MESH,
        )

    def arrived(block, k):
        copy(SIDE, held.at[block], block, k).wait_recv()

    def product(source, block):
        schur[block] = front[block] - lax.dot_general(
            source[...], panel[...], (((1,), (1,)), ((), ())),
            preferred_element_type=jnp.float32,
        )

    for k in range(chunks):
        pl.when(above)(lambda: copy(UP, panel, f, k).start())
        pl.when(below)(lambda: copy(DOWN, panel, f, k).start())
    for k in range(chunks):
        copy(SIDE, panel, f, k).start()
    product(panel, f)
    for k in range(chunks):
        arrived(side, k)
    product(held.at[side], side)

    def step(s, carry):
        lo, hi = z - 1 - s, z + 1 + s
        for k in range(chunks):
            @pl.when(lo >= 0)
            def _():
                b = lo * 2 + c
                arrived(b, k)
                pl.when(above)(lambda: copy(UP, held.at[b], b, k).start())
                copy(SIDE, held.at[b], b, k).start()

            @pl.when(hi < nz)
            def _():
                b = hi * 2 + c
                arrived(b, k)
                pl.when(below)(lambda: copy(DOWN, held.at[b], b, k).start())
                copy(SIDE, held.at[b], b, k).start()

        for far, there in ((lo, lo >= 0), (hi, hi < nz)):
            @pl.when(there)
            def _():
                product(held.at[far * 2 + c], far * 2 + c)

        for far, there in ((lo, lo >= 0), (hi, hi < nz)):
            @pl.when(there)
            def _():
                b = far * 2 + 1 - c
                for k in range(chunks):
                    arrived(b, k)
                product(held.at[b], b)
        return carry

    lax.fori_loop(0, nz - 1, step, 0)

    def pick(d):
        row, present = jnp.int32(0), jnp.int32(0)
        for i in range(blocks):
            hit = targets[0, i] == d
            row = jnp.where(hit, i, row)
            present = jnp.where(hit, 1, present)
        tile = schur[row]
        return jnp.where(present > 0, tile, jnp.zeros_like(tile))

    def leaf_copy(j):
        return pltpu.make_async_remote_copy(
            src_ref=message.at[j],
            dst_ref=received.at[leaf],
            send_sem=leaf_send.at[j],
            recv_sem=leaf_recv.at[leaf],
            device_id=((leaf + j) % n_leaf, f),
            device_id_type=MESH,
        )

    for j in range(1, n_leaf):
        message[j] = pick((leaf + j) % n_leaf)
        leaf_copy(j).start()
    received[leaf] = pick(leaf)

    def settle(block, forwards_up, forwards_down):
        for k in range(chunks):
            pl.when(forwards_up)(lambda: copy(UP, panel, block, k).wait_send())
            pl.when(forwards_down)(lambda: copy(DOWN, panel, block, k).wait_send())
            copy(SIDE, panel, block, k).wait_send()

    settle(f, above, below)

    def settle_step(s, carry):
        lo, hi = z - 1 - s, z + 1 + s
        pl.when(lo >= 0)(lambda: settle(lo * 2 + c, above, False))
        pl.when(hi < nz)(lambda: settle(hi * 2 + c, False, below))
        return carry

    lax.fori_loop(0, nz - 1, settle_step, 0)

    for j in range(1, n_leaf):
        g = (leaf + n_leaf - j) % n_leaf
        pltpu.make_async_remote_copy(
            src_ref=message.at[j],
            dst_ref=received.at[g],
            send_sem=leaf_send.at[j],
            recv_sem=leaf_recv.at[g],
            device_id=((leaf + j) % n_leaf, f),
            device_id_type=MESH,
        ).wait_recv()
    for a in range(out.shape[0]):
        total = ancestor[a]
        for g in range(n_leaf):
            tile = received[g]
            total = total + jnp.where(extend[0, g] == a, tile, jnp.zeros_like(tile))
        out[a] = total
    for j in range(1, n_leaf):
        leaf_copy(j).wait_send()


def shards(factored_panel, front_tiles, ancestor_tiles, send_slots, extend_slots):
    n_leaf = lax.axis_size("leaf")
    n_front = lax.axis_size("front")
    nz = n_front // 2
    chunks = max(1, 16 // nz)
    blocks, tile_size = front_tiles.shape[0], front_tiles.shape[1]
    rows, width = factored_panel.shape
    vmem = pl.BlockSpec(memory_space=pltpu.VMEM)
    smem = pl.BlockSpec(memory_space=pltpu.SMEM)
    return pl.pallas_call(
        functools.partial(kernel, nz, n_leaf, chunks),
        out_shape=jax.ShapeDtypeStruct(ancestor_tiles.shape, jnp.float32),
        in_specs=[vmem, vmem, vmem, smem, smem],
        out_specs=vmem,
        scratch_shapes=[
            pltpu.VMEM((n_front, rows, width), jnp.bfloat16),
            pltpu.VMEM((blocks, tile_size, tile_size), jnp.float32),
            pltpu.VMEM((n_leaf, tile_size, tile_size), jnp.float32),
            pltpu.VMEM((n_leaf, tile_size, tile_size), jnp.float32),
            pltpu.SemaphoreType.DMA((3, n_front, chunks)),
            pltpu.SemaphoreType.DMA((n_front, chunks)),
            pltpu.SemaphoreType.DMA((n_leaf,)),
            pltpu.SemaphoreType.DMA((n_leaf,)),
        ],
        compiler_params=pltpu.CompilerParams(
            collective_id=0, has_side_effects=True, vmem_limit_bytes=40 * 1024 * 1024
        ),
        cost_estimate=pl.CostEstimate(
            flops=2 * blocks * tile_size * rows * width,
            bytes_accessed=2 * n_front * rows * width,
            transcendentals=0,
        ),
    )(factored_panel, front_tiles, ancestor_tiles, send_slots, extend_slots)


def solution(mesh):
    placed = (
        P(("leaf", "front"), None),
        P(("leaf", "front"), None, None),
        P(("leaf", "front"), None, None),
        P(("leaf", "front"), None),
        P(("leaf", "front"), None),
    )
    return jax.shard_map(
        shards,
        mesh=mesh,
        in_specs=placed,
        out_specs=P(("leaf", "front"), None, None),
        check_vma=False,
    )
```

```python
import functools

import jax
import jax.numpy as jnp
from jax import lax
from jax.experimental import pallas as pl
from jax.experimental.pallas import tpu as pltpu
from jax.sharding import PartitionSpec as P

MESH = pl.DeviceIdType.MESH
UP, DOWN, SIDE = 0, 1, 2
ACROSS, MATE = 0, 1


def kernel(nz, n_leaf, chunks, panel_hbm, front_hbm, ancestor_hbm, targets_hbm, extend_hbm, out,
           pair, front, ancestor, targets, extend, held, schur, made, taken, message, received,
           load_sem, send_sem, recv_sem, tile_send, tile_recv, leaf_send, leaf_recv):
    leaf = lax.axis_index("leaf")
    f = lax.axis_index("front")
    z, c = f // 2, f % 2
    side = f + 1 - 2 * c
    below, above = z > 0, z < nz - 1
    size = panel_hbm.shape[0]
    rows = size // chunks
    blocks = schur.shape[0]
    panel = pair.at[pl.ds(0, size)]
    loads = [
        pltpu.make_async_copy(source, to, load_sem.at[n])
        for n, (source, to) in enumerate((
            (panel_hbm, panel), (front_hbm, front), (ancestor_hbm, ancestor),
            (targets_hbm, targets), (extend_hbm, extend),
        ))
    ]
    for load in loads:
        load.start()

    barrier = pltpu.get_barrier_semaphore()

    def greet(device):
        pl.semaphore_signal(barrier, inc=1, device_id=device, device_id_type=MESH)

    pl.when(below)(lambda: greet((leaf, f - 2)))
    pl.when(above)(lambda: greet((leaf, f + 2)))
    greet((leaf, side))
    for j in range(1, n_leaf):
        greet(((leaf + j) % n_leaf, f))
    pl.semaphore_wait(
        barrier, n_leaf + below.astype(jnp.int32) + above.astype(jnp.int32)
    )

    def piece(ref, k):
        return ref.at[pl.ds(k * rows, rows)]

    def copy(way, source, block, k):
        to = {UP: f + 2, DOWN: f - 2, SIDE: side}[way]
        return pltpu.make_async_remote_copy(
            src_ref=piece(source, k),
            dst_ref=piece(held.at[block], k),
            send_sem=send_sem.at[way, block, k],
            recv_sem=recv_sem.at[block, k],
            device_id=(leaf, to),
            device_id_type=MESH,
        )

    def arrived(block, k):
        copy(SIDE, held.at[block], block, k).wait_recv()

    def product(source, block):
        schur[block] = front[block] - lax.dot_general(
            source[...], panel[...], (((1,), (1,)), ((), ())),
            preferred_element_type=jnp.float32,
        )

    loads[0].wait()
    loads[1].wait()

    def relay():
        for k in range(chunks):
            pl.when(above)(lambda: copy(UP, panel, f, k).start())
            pl.when(below)(lambda: copy(DOWN, panel, f, k).start())
        for k in range(chunks):
            copy(SIDE, panel, f, k).start()
        product(panel, f)
        for k in range(chunks):
            arrived(side, k)
        product(held.at[side], side)

        def step(s, carry):
            lo, hi = z - 1 - s, z + 1 + s
            for k in range(chunks):
                @pl.when(lo >= 0)
                def _():
                    b = lo * 2 + c
                    arrived(b, k)
                    pl.when(above)(lambda: copy(UP, held.at[b], b, k).start())
                    copy(SIDE, held.at[b], b, k).start()

                @pl.when(hi < nz)
                def _():
                    b = hi * 2 + c
                    arrived(b, k)
                    pl.when(below)(lambda: copy(DOWN, held.at[b], b, k).start())
                    copy(SIDE, held.at[b], b, k).start()

            for far, there in ((lo, lo >= 0), (hi, hi < nz)):
                @pl.when(there)
                def _():
                    product(held.at[far * 2 + c], far * 2 + c)

            for far, there in ((lo, lo >= 0), (hi, hi < nz)):
                @pl.when(there)
                def _():
                    b = far * 2 + 1 - c
                    for k in range(chunks):
                        arrived(b, k)
                    product(held.at[b], b)
            return carry

        lax.fori_loop(0, nz - 1, step, 0)

    def relay_settle():
        def settle(block, forwards_up, forwards_down):
            for k in range(chunks):
                pl.when(forwards_up)(lambda: copy(UP, panel, block, k).wait_send())
                pl.when(forwards_down)(lambda: copy(DOWN, panel, block, k).wait_send())
                copy(SIDE, panel, block, k).wait_send()

        settle(f, above, below)

        def settle_step(s, carry):
            lo, hi = z - 1 - s, z + 1 + s
            pl.when(lo >= 0)(lambda: settle(lo * 2 + c, above, False))
            pl.when(hi < nz)(lambda: settle(hi * 2 + c, False, below))
            return carry

        lax.fori_loop(0, nz - 1, settle_step, 0)

    mate, across = z + 1 - 2 * (z % 2), nz - 1 - z
    inner = (z > 0) & (z < nz - 1)
    pieces = 2
    tall = size // pieces

    def pass_on(way, source, block, k):
        to = {ACROSS: across * 2 + c, MATE: mate * 2 + c, SIDE: side}[way]
        return pltpu.make_async_remote_copy(
            src_ref=piece(source, k),
            dst_ref=piece(held.at[block], k),
            send_sem=send_sem.at[way, block, k],
            recv_sem=recv_sem.at[block, k],
            device_id=(leaf, to),
            device_id_type=MESH,
        )

    def tile_copy(block, n):
        return pltpu.make_async_remote_copy(
            src_ref=made.at[block, pl.ds(n * tall, tall)],
            dst_ref=taken.at[block, pl.ds(n * tall, tall)],
            send_sem=tile_send.at[block, n],
            recv_sem=tile_recv.at[block, n],
            device_id=(leaf, mate * 2 + c),
            device_id_type=MESH,
        )

    def both(block, n):
        at = pl.ds(n * tall, tall)
        result = lax.dot_general(
            held[block, at], pair[...], (((1,), (1,)), ((), ())),
            preferred_element_type=jnp.float32,
        )
        made[block, at] = result[:, size:]
        tile_copy(block, n).start()
        schur[block, at] = front[block, at] - result[:, :size]

    far_inner, far_outer = across, nz - 1 - mate

    def inner_start():
        for k in range(chunks):
            pass_on(ACROSS, panel, f, k).start()
            pass_on(MATE, panel, f, k).start()
        for k in range(chunks):
            pass_on(SIDE, panel, f, k).start()
        product(panel, f)
        for k in range(chunks):
            arrived(side, k)
        product(held.at[side], side)
        near, far = mate * 2 + c, far_inner * 2 + c
        for k in range(chunks):
            arrived(near, k)
            pass_on(ACROSS, held.at[near], near, k).start()
            pass_on(SIDE, held.at[near], near, k).start()
            arrived(far, k)
            pass_on(SIDE, held.at[far], far, k).start()
        pair[pl.ds(size, size)] = held[near]
        for n in range(pieces):
            both(far, n)
        far = far_inner * 2 + 1 - c
        for k in range(chunks):
            arrived(far, k)
        for n in range(pieces):
            both(far, n)
        product(held.at[near], near)
        near = mate * 2 + 1 - c
        for k in range(chunks):
            arrived(near, k)
        product(held.at[near], near)
        far, other = far_outer * 2 + c, far_outer * 2 + 1 - c
        for n in range(pieces):
            part = range(n * chunks // pieces, (n + 1) * chunks // pieces)
            for k in part:
                arrived(far, k)
                pass_on(SIDE, held.at[far], far, k).start()
            both(far, n)
            for k in part:
                arrived(other, k)
            both(other, n)

    def outer_start():
        for k in range(chunks):
            pass_on(MATE, panel, f, k).start()
        for k in range(chunks):
            pass_on(SIDE, panel, f, k).start()
        product(panel, f)
        for k in range(chunks):
            arrived(side, k)
        product(held.at[side], side)
        near, other = mate * 2 + c, mate * 2 + 1 - c
        for k in range(chunks):
            arrived(near, k)
            pass_on(SIDE, held.at[near], near, k).start()
        product(held.at[near], near)
        for k in range(chunks):
            arrived(other, k)
        product(held.at[other], other)
        for there in (far_outer, far_inner):
            for n in range(pieces):
                at = pl.ds(n * tall, tall)
                for b in (there * 2 + c, there * 2 + 1 - c):
                    tile_copy(b, n).wait_recv()
                    schur[b, at] = front[b, at] - taken[b, at]

    def inner_settle():
        for k in range(chunks):
            for way in (ACROSS, MATE, SIDE):
                pass_on(way, panel, f, k).wait_send()
            for way in (ACROSS, SIDE):
                pass_on(way, panel, mate * 2 + c, k).wait_send()
            pass_on(SIDE, panel, far_inner * 2 + c, k).wait_send()
            pass_on(SIDE, panel, far_outer * 2 + c, k).wait_send()
        for there in (far_outer, far_inner):
            for n in range(pieces):
                for b in (there * 2, there * 2 + 1):
                    tile_copy(b, n).wait_send()

    def outer_settle():
        for k in range(chunks):
            pass_on(MATE, panel, f, k).wait_send()
            pass_on(SIDE, panel, f, k).wait_send()
            pass_on(SIDE, panel, mate * 2 + c, k).wait_send()

    halves = nz == 4
    if halves:
        pl.when(inner)(inner_start)
        pl.when(jnp.logical_not(inner))(outer_start)
    else:
        relay()

    loads[3].wait()

    def pick(d):
        row, present = jnp.int32(0), jnp.int32(0)
        for i in range(blocks):
            hit = targets[0, i] == d
            row = jnp.where(hit, i, row)
            present = jnp.where(hit, 1, present)
        tile = schur[row]
        return jnp.where(present > 0, tile, jnp.zeros_like(tile))

    def leaf_copy(j):
        return pltpu.make_async_remote_copy(
            src_ref=message.at[j],
            dst_ref=received.at[leaf],
            send_sem=leaf_send.at[j],
            recv_sem=leaf_recv.at[leaf],
            device_id=((leaf + j) % n_leaf, f),
            device_id_type=MESH,
        )

    for j in range(1, n_leaf):
        message[j] = pick((leaf + j) % n_leaf)
        leaf_copy(j).start()
    received[leaf] = pick(leaf)

    if halves:
        pl.when(inner)(inner_settle)
        pl.when(jnp.logical_not(inner))(outer_settle)
    else:
        relay_settle()
    loads[2].wait()
    loads[4].wait()

    for j in range(1, n_leaf):
        g = (leaf + n_leaf - j) % n_leaf
        pltpu.make_async_remote_copy(
            src_ref=message.at[j],
            dst_ref=received.at[g],
            send_sem=leaf_send.at[j],
            recv_sem=leaf_recv.at[g],
            device_id=((leaf + j) % n_leaf, f),
            device_id_type=MESH,
        ).wait_recv()
    for a in range(out.shape[0]):
        total = ancestor[a]
        for g in range(n_leaf):
            tile = received[g]
            total = total + jnp.where(extend[0, g] == a, tile, jnp.zeros_like(tile))
        out[a] = total
    for j in range(1, n_leaf):
        leaf_copy(j).wait_send()


def shards(factored_panel, front_tiles, ancestor_tiles, send_slots, extend_slots):
    n_leaf = lax.axis_size("leaf")
    n_front = lax.axis_size("front")
    nz = n_front // 2
    chunks = max(1, 16 // nz)
    blocks, tile_size = front_tiles.shape[0], front_tiles.shape[1]
    rows, width = factored_panel.shape
    vmem = pl.BlockSpec(memory_space=pltpu.VMEM)
    hbm = pl.BlockSpec(memory_space=pltpu.HBM)
    return pl.pallas_call(
        functools.partial(kernel, nz, n_leaf, chunks),
        out_shape=jax.ShapeDtypeStruct(ancestor_tiles.shape, jnp.float32),
        in_specs=[hbm] * 5,
        out_specs=vmem,
        scratch_shapes=[
            pltpu.VMEM((2 * rows, width), jnp.bfloat16),
            pltpu.VMEM(front_tiles.shape, jnp.float32),
            pltpu.VMEM(ancestor_tiles.shape, jnp.float32),
            pltpu.SMEM(send_slots.shape, jnp.int32),
            pltpu.SMEM(extend_slots.shape, jnp.int32),
            pltpu.VMEM((n_front, rows, width), jnp.bfloat16),
            pltpu.VMEM((blocks, tile_size, tile_size), jnp.float32),
            pltpu.VMEM((blocks, tile_size, tile_size), jnp.float32),
            pltpu.VMEM((blocks, tile_size, tile_size), jnp.float32),
            pltpu.VMEM((n_leaf, tile_size, tile_size), jnp.float32),
            pltpu.VMEM((n_leaf, tile_size, tile_size), jnp.float32),
            pltpu.SemaphoreType.DMA((5,)),
            pltpu.SemaphoreType.DMA((3, n_front, chunks)),
            pltpu.SemaphoreType.DMA((n_front, chunks)),
            pltpu.SemaphoreType.DMA((blocks, 2)),
            pltpu.SemaphoreType.DMA((blocks, 2)),
            pltpu.SemaphoreType.DMA((n_leaf,)),
            pltpu.SemaphoreType.DMA((n_leaf,)),
        ],
        compiler_params=pltpu.CompilerParams(
            collective_id=0, has_side_effects=True, vmem_limit_bytes=63 * 1024 * 1024
        ),
        cost_estimate=pl.CostEstimate(
            flops=2 * blocks * tile_size * rows * width,
            bytes_accessed=2 * n_front * rows * width,
            transcendentals=0,
        ),
    )(factored_panel, front_tiles, ancestor_tiles, send_slots, extend_slots)


def solution(mesh):
    placed = (
        P(("leaf", "front"), None),
        P(("leaf", "front"), None, None),
        P(("leaf", "front"), None, None),
        P(("leaf", "front"), None),
        P(("leaf", "front"), None),
    )
    return jax.shard_map(
        shards,
        mesh=mesh,
        in_specs=placed,
        out_specs=P(("leaf", "front"), None, None),
        check_vma=False,
    )
```

```python
import functools

import jax
import jax.numpy as jnp
from jax import lax
from jax.experimental import pallas as pl
from jax.experimental.pallas import tpu as pltpu
from jax.sharding import PartitionSpec as P

MESH = pl.DeviceIdType.MESH
UP, DOWN, SIDE = 0, 1, 2
ACROSS, MATE = 0, 1


def kernel(nz, n_leaf, chunks, panel_hbm, front_hbm, targets_hbm, received,
           pair, front, targets, held, schur, made, taken, message,
           load_sem, send_sem, recv_sem, tile_send, tile_recv, leaf_send, leaf_recv):
    leaf = lax.axis_index("leaf")
    f = lax.axis_index("front")
    z, c = f // 2, f % 2
    side = f + 1 - 2 * c
    below, above = z > 0, z < nz - 1
    size = panel_hbm.shape[0]
    rows = size // chunks
    blocks = schur.shape[0]
    panel = pair.at[pl.ds(0, size)]
    loads = [
        pltpu.make_async_copy(source, to, load_sem.at[n])
        for n, (source, to) in enumerate((
            (panel_hbm, panel), (front_hbm, front), (targets_hbm, targets),
        ))
    ]
    for load in loads:
        load.start()

    barrier = pltpu.get_barrier_semaphore()

    def greet(device):
        pl.semaphore_signal(barrier, inc=1, device_id=device, device_id_type=MESH)

    pl.when(below)(lambda: greet((leaf, f - 2)))
    pl.when(above)(lambda: greet((leaf, f + 2)))
    greet((leaf, side))
    for j in range(1, n_leaf):
        greet(((leaf + j) % n_leaf, f))
    pl.semaphore_wait(
        barrier, n_leaf + below.astype(jnp.int32) + above.astype(jnp.int32)
    )

    def piece(ref, k):
        return ref.at[pl.ds(k * rows, rows)]

    def copy(way, source, block, k):
        to = {UP: f + 2, DOWN: f - 2, SIDE: side}[way]
        return pltpu.make_async_remote_copy(
            src_ref=piece(source, k),
            dst_ref=piece(held.at[block], k),
            send_sem=send_sem.at[way, block, k],
            recv_sem=recv_sem.at[block, k],
            device_id=(leaf, to),
            device_id_type=MESH,
        )

    def arrived(block, k):
        copy(SIDE, held.at[block], block, k).wait_recv()

    def product(source, block):
        schur[block] = front[block] - lax.dot_general(
            source[...], panel[...], (((1,), (1,)), ((), ())),
            preferred_element_type=jnp.float32,
        )

    loads[0].wait()
    loads[1].wait()

    def relay():
        for k in range(chunks):
            pl.when(above)(lambda: copy(UP, panel, f, k).start())
            pl.when(below)(lambda: copy(DOWN, panel, f, k).start())
        for k in range(chunks):
            copy(SIDE, panel, f, k).start()
        product(panel, f)
        for k in range(chunks):
            arrived(side, k)
        product(held.at[side], side)

        def step(s, carry):
            lo, hi = z - 1 - s, z + 1 + s
            for k in range(chunks):
                @pl.when(lo >= 0)
                def _():
                    b = lo * 2 + c
                    arrived(b, k)
                    pl.when(above)(lambda: copy(UP, held.at[b], b, k).start())
                    copy(SIDE, held.at[b], b, k).start()

                @pl.when(hi < nz)
                def _():
                    b = hi * 2 + c
                    arrived(b, k)
                    pl.when(below)(lambda: copy(DOWN, held.at[b], b, k).start())
                    copy(SIDE, held.at[b], b, k).start()

            for far, there in ((lo, lo >= 0), (hi, hi < nz)):
                @pl.when(there)
                def _():
                    product(held.at[far * 2 + c], far * 2 + c)

            for far, there in ((lo, lo >= 0), (hi, hi < nz)):
                @pl.when(there)
                def _():
                    b = far * 2 + 1 - c
                    for k in range(chunks):
                        arrived(b, k)
                    product(held.at[b], b)
            return carry

        lax.fori_loop(0, nz - 1, step, 0)

    def relay_settle():
        def settle(block, forwards_up, forwards_down):
            for k in range(chunks):
                pl.when(forwards_up)(lambda: copy(UP, panel, block, k).wait_send())
                pl.when(forwards_down)(lambda: copy(DOWN, panel, block, k).wait_send())
                copy(SIDE, panel, block, k).wait_send()

        settle(f, above, below)

        def settle_step(s, carry):
            lo, hi = z - 1 - s, z + 1 + s
            pl.when(lo >= 0)(lambda: settle(lo * 2 + c, above, False))
            pl.when(hi < nz)(lambda: settle(hi * 2 + c, False, below))
            return carry

        lax.fori_loop(0, nz - 1, settle_step, 0)

    mate, across = z + 1 - 2 * (z % 2), nz - 1 - z
    inner = (z > 0) & (z < nz - 1)
    pieces = 2
    tall = size // pieces

    def pass_on(way, source, block, k):
        to = {ACROSS: across * 2 + c, MATE: mate * 2 + c, SIDE: side}[way]
        return pltpu.make_async_remote_copy(
            src_ref=piece(source, k),
            dst_ref=piece(held.at[block], k),
            send_sem=send_sem.at[way, block, k],
            recv_sem=recv_sem.at[block, k],
            device_id=(leaf, to),
            device_id_type=MESH,
        )

    def tile_copy(block, n):
        return pltpu.make_async_remote_copy(
            src_ref=made.at[block, pl.ds(n * tall, tall)],
            dst_ref=taken.at[block, pl.ds(n * tall, tall)],
            send_sem=tile_send.at[block, n],
            recv_sem=tile_recv.at[block, n],
            device_id=(leaf, mate * 2 + c),
            device_id_type=MESH,
        )

    def both(block, n):
        at = pl.ds(n * tall, tall)
        result = lax.dot_general(
            held[block, at], pair[...], (((1,), (1,)), ((), ())),
            preferred_element_type=jnp.float32,
        )
        made[block, at] = result[:, size:]
        tile_copy(block, n).start()
        schur[block, at] = front[block, at] - result[:, :size]

    far_inner, far_outer = across, nz - 1 - mate

    def inner_start():
        for k in range(chunks):
            pass_on(ACROSS, panel, f, k).start()
        for k in range(chunks):
            pass_on(SIDE, panel, f, k).start()
        for k in range(chunks):
            pass_on(MATE, panel, f, k).start()
        product(panel, f)
        for k in range(chunks):
            arrived(side, k)
        product(held.at[side], side)
        near, far = mate * 2 + c, far_inner * 2 + c
        for k in range(chunks):
            arrived(near, k)
            pass_on(ACROSS, held.at[near], near, k).start()
            pass_on(SIDE, held.at[near], near, k).start()
            arrived(far, k)
            pass_on(SIDE, held.at[far], far, k).start()
        pair[pl.ds(size, size)] = held[near]
        for n in range(pieces):
            both(far, n)
        far = far_inner * 2 + 1 - c
        for k in range(chunks):
            arrived(far, k)
        for n in range(pieces):
            both(far, n)
        product(held.at[near], near)
        near = mate * 2 + 1 - c
        for k in range(chunks):
            arrived(near, k)
        product(held.at[near], near)
        far, other = far_outer * 2 + c, far_outer * 2 + 1 - c
        for n in range(pieces):
            part = range(n * chunks // pieces, (n + 1) * chunks // pieces)
            for k in part:
                arrived(far, k)
                pass_on(SIDE, held.at[far], far, k).start()
            both(far, n)
            for k in part:
                arrived(other, k)
            both(other, n)

    def outer_start():
        for k in range(chunks):
            pass_on(MATE, panel, f, k).start()
        for k in range(chunks):
            pass_on(SIDE, panel, f, k).start()
        product(panel, f)
        for k in range(chunks):
            arrived(side, k)
        product(held.at[side], side)
        near, other = mate * 2 + c, mate * 2 + 1 - c
        for k in range(chunks):
            arrived(near, k)
            pass_on(SIDE, held.at[near], near, k).start()
        product(held.at[near], near)
        for k in range(chunks):
            arrived(other, k)
        product(held.at[other], other)
        for there in (far_outer, far_inner):
            for n in range(pieces):
                at = pl.ds(n * tall, tall)
                for b in (there * 2 + c, there * 2 + 1 - c):
                    tile_copy(b, n).wait_recv()
                    schur[b, at] = front[b, at] - taken[b, at]

    def inner_settle():
        for k in range(chunks):
            for way in (ACROSS, MATE, SIDE):
                pass_on(way, panel, f, k).wait_send()
            for way in (ACROSS, SIDE):
                pass_on(way, panel, mate * 2 + c, k).wait_send()
            pass_on(SIDE, panel, far_inner * 2 + c, k).wait_send()
            pass_on(SIDE, panel, far_outer * 2 + c, k).wait_send()
        for there in (far_outer, far_inner):
            for n in range(pieces):
                for b in (there * 2, there * 2 + 1):
                    tile_copy(b, n).wait_send()

    def outer_settle():
        for k in range(chunks):
            pass_on(MATE, panel, f, k).wait_send()
            pass_on(SIDE, panel, f, k).wait_send()
            pass_on(SIDE, panel, mate * 2 + c, k).wait_send()

    halves = nz == 4
    if halves:
        pl.when(inner)(inner_start)
        pl.when(jnp.logical_not(inner))(outer_start)
    else:
        relay()

    loads[2].wait()

    def pick(d):
        row, present = jnp.int32(0), jnp.int32(0)
        for i in range(blocks):
            hit = targets[0, i] == d
            row = jnp.where(hit, i, row)
            present = jnp.where(hit, 1, present)
        tile = schur[row]
        return jnp.where(present > 0, tile, jnp.zeros_like(tile))

    def leaf_copy(j):
        return pltpu.make_async_remote_copy(
            src_ref=message.at[j],
            dst_ref=received.at[leaf],
            send_sem=leaf_send.at[j],
            recv_sem=leaf_recv.at[leaf],
            device_id=((leaf + j) % n_leaf, f),
            device_id_type=MESH,
        )

    for j in range(1, n_leaf):
        message[j] = pick((leaf + j) % n_leaf)
        leaf_copy(j).start()
    message[0] = pick(leaf)
    keep = pltpu.make_async_copy(message.at[0], received.at[leaf], leaf_recv.at[leaf])
    keep.start()

    if halves:
        pl.when(inner)(inner_settle)
        pl.when(jnp.logical_not(inner))(outer_settle)
    else:
        relay_settle()
    for j in range(1, n_leaf):
        g = (leaf + n_leaf - j) % n_leaf
        pltpu.make_async_remote_copy(
            src_ref=message.at[j],
            dst_ref=received.at[g],
            send_sem=leaf_send.at[j],
            recv_sem=leaf_recv.at[g],
            device_id=((leaf + j) % n_leaf, f),
            device_id_type=MESH,
        ).wait_recv()
    keep.wait()
    for j in range(1, n_leaf):
        leaf_copy(j).wait_send()


def extend_add(ancestor, received, extend, out):
    first = pl.program_id(0) * out.shape[0]
    out[...] = ancestor[...]
    for g in range(received.shape[0]):
        slot = extend[0, g] - first

        @pl.when((slot >= 0) & (slot < out.shape[0]))
        def _():
            out[slot] += received[g]


def shards(factored_panel, front_tiles, ancestor_tiles, send_slots, extend_slots):
    n_leaf = lax.axis_size("leaf")
    n_front = lax.axis_size("front")
    nz = n_front // 2
    chunks = max(1, 8 // nz)
    blocks, tile_size = front_tiles.shape[0], front_tiles.shape[1]
    rows, width = factored_panel.shape
    hbm = pl.BlockSpec(memory_space=pltpu.HBM)
    received = pl.pallas_call(
        functools.partial(kernel, nz, n_leaf, chunks),
        out_shape=jax.ShapeDtypeStruct((n_leaf, tile_size, tile_size), jnp.float32),
        in_specs=[hbm] * 3,
        out_specs=hbm,
        scratch_shapes=[
            pltpu.VMEM((2 * rows, width), jnp.bfloat16),
            pltpu.VMEM(front_tiles.shape, jnp.float32),
            pltpu.SMEM(send_slots.shape, jnp.int32),
            pltpu.VMEM((n_front, rows, width), jnp.bfloat16),
            pltpu.VMEM((blocks, tile_size, tile_size), jnp.float32),
            pltpu.VMEM((blocks, tile_size, tile_size), jnp.float32),
            pltpu.VMEM((blocks, tile_size, tile_size), jnp.float32),
            pltpu.VMEM((n_leaf, tile_size, tile_size), jnp.float32),
            pltpu.SemaphoreType.DMA((3,)),
            pltpu.SemaphoreType.DMA((3, n_front, chunks)),
            pltpu.SemaphoreType.DMA((n_front, chunks)),
            pltpu.SemaphoreType.DMA((blocks, 2)),
            pltpu.SemaphoreType.DMA((blocks, 2)),
            pltpu.SemaphoreType.DMA((n_leaf,)),
            pltpu.SemaphoreType.DMA((n_leaf,)),
        ],
        compiler_params=pltpu.CompilerParams(
            collective_id=0, has_side_effects=True, vmem_limit_bytes=63 * 1024 * 1024
        ),
        cost_estimate=pl.CostEstimate(
            flops=2 * blocks * tile_size * rows * width,
            bytes_accessed=2 * n_front * rows * width,
            transcendentals=0,
        ),
    )(factored_panel, front_tiles, send_slots)
    held = ancestor_tiles.shape[0]
    group = held // 2 if held % 2 == 0 else held
    part = pl.BlockSpec((group, tile_size, tile_size), lambda n: (n, 0, 0))
    return pl.pallas_call(
        extend_add,
        grid=(held // group,),
        out_shape=jax.ShapeDtypeStruct(ancestor_tiles.shape, jnp.float32),
        in_specs=[
            part,
            pl.BlockSpec((n_leaf, tile_size, tile_size), lambda n: (0, 0, 0)),
            pl.BlockSpec(memory_space=pltpu.SMEM),
        ],
        out_specs=part,
    )(ancestor_tiles, received, extend_slots)


def solution(mesh):
    placed = (
        P(("leaf", "front"), None),
        P(("leaf", "front"), None, None),
        P(("leaf", "front"), None, None),
        P(("leaf", "front"), None),
        P(("leaf", "front"), None),
    )
    return jax.shard_map(
        shards,
        mesh=mesh,
        in_specs=placed,
        out_specs=P(("leaf", "front"), None, None),
        check_vma=False,
    )
```

```python
import functools

import jax
import jax.numpy as jnp
from jax import lax
from jax.experimental import pallas as pl
from jax.experimental.pallas import tpu as pltpu
from jax.sharding import PartitionSpec as P

MESH = pl.DeviceIdType.MESH
UP, DOWN, SIDE = 0, 1, 2
ACROSS, MATE = 0, 1


def kernel(nz, n_leaf, chunks, panel_hbm, front_hbm, targets_hbm, received,
           pair, front, targets, held, schur, made, taken, message,
           load_sem, send_sem, recv_sem, tile_send, tile_recv, leaf_send, leaf_recv):
    leaf = lax.axis_index("leaf")
    f = lax.axis_index("front")
    z, c = f // 2, f % 2
    side = f + 1 - 2 * c
    below, above = z > 0, z < nz - 1
    size = panel_hbm.shape[0]
    rows = size // chunks
    blocks = schur.shape[0]
    panel = pair.at[pl.ds(0, size)]
    loads = [
        pltpu.make_async_copy(source, to, load_sem.at[n])
        for n, (source, to) in enumerate((
            (panel_hbm, panel), (front_hbm, front), (targets_hbm, targets),
        ))
    ]
    for load in loads:
        load.start()

    barrier = pltpu.get_barrier_semaphore()

    def greet(device):
        pl.semaphore_signal(barrier, inc=1, device_id=device, device_id_type=MESH)

    pl.when(below)(lambda: greet((leaf, f - 2)))
    pl.when(above)(lambda: greet((leaf, f + 2)))
    greet((leaf, side))
    for j in range(1, n_leaf):
        greet(((leaf + j) % n_leaf, f))
    pl.semaphore_wait(
        barrier, n_leaf + below.astype(jnp.int32) + above.astype(jnp.int32)
    )

    def piece(ref, k):
        return ref.at[pl.ds(k * rows, rows)]

    def copy(way, source, block, k):
        to = {UP: f + 2, DOWN: f - 2, SIDE: side}[way]
        return pltpu.make_async_remote_copy(
            src_ref=piece(source, k),
            dst_ref=piece(held.at[block], k),
            send_sem=send_sem.at[way, block, k],
            recv_sem=recv_sem.at[block, k],
            device_id=(leaf, to),
            device_id_type=MESH,
        )

    def arrived(block, k):
        copy(SIDE, held.at[block], block, k).wait_recv()

    def product(source, block):
        schur[block] = front[block] - lax.dot_general(
            source[...], panel[...], (((1,), (1,)), ((), ())),
            preferred_element_type=jnp.float32,
        )

    loads[0].wait()
    loads[1].wait()

    def relay():
        for k in range(chunks):
            pl.when(above)(lambda: copy(UP, panel, f, k).start())
            pl.when(below)(lambda: copy(DOWN, panel, f, k).start())
        for k in range(chunks):
            copy(SIDE, panel, f, k).start()
        product(panel, f)
        for k in range(chunks):
            arrived(side, k)
        product(held.at[side], side)

        def step(s, carry):
            lo, hi = z - 1 - s, z + 1 + s
            for k in range(chunks):
                @pl.when(lo >= 0)
                def _():
                    b = lo * 2 + c
                    arrived(b, k)
                    pl.when(above)(lambda: copy(UP, held.at[b], b, k).start())
                    copy(SIDE, held.at[b], b, k).start()

                @pl.when(hi < nz)
                def _():
                    b = hi * 2 + c
                    arrived(b, k)
                    pl.when(below)(lambda: copy(DOWN, held.at[b], b, k).start())
                    copy(SIDE, held.at[b], b, k).start()

            for far, there in ((lo, lo >= 0), (hi, hi < nz)):
                @pl.when(there)
                def _():
                    product(held.at[far * 2 + c], far * 2 + c)

            for far, there in ((lo, lo >= 0), (hi, hi < nz)):
                @pl.when(there)
                def _():
                    b = far * 2 + 1 - c
                    for k in range(chunks):
                        arrived(b, k)
                    product(held.at[b], b)
            return carry

        lax.fori_loop(0, nz - 1, step, 0)

    def relay_settle():
        def settle(block, forwards_up, forwards_down):
            for k in range(chunks):
                pl.when(forwards_up)(lambda: copy(UP, panel, block, k).wait_send())
                pl.when(forwards_down)(lambda: copy(DOWN, panel, block, k).wait_send())
                copy(SIDE, panel, block, k).wait_send()

        settle(f, above, below)

        def settle_step(s, carry):
            lo, hi = z - 1 - s, z + 1 + s
            pl.when(lo >= 0)(lambda: settle(lo * 2 + c, above, False))
            pl.when(hi < nz)(lambda: settle(hi * 2 + c, False, below))
            return carry

        lax.fori_loop(0, nz - 1, settle_step, 0)

    mate, across = z + 1 - 2 * (z % 2), nz - 1 - z
    inner = (z > 0) & (z < nz - 1)
    pieces = 2
    tall = size // pieces

    def pass_on(way, source, block, k):
        to = {ACROSS: across * 2 + c, MATE: mate * 2 + c, SIDE: side}[way]
        return pltpu.make_async_remote_copy(
            src_ref=piece(source, k),
            dst_ref=piece(held.at[block], k),
            send_sem=send_sem.at[way, block, k],
            recv_sem=recv_sem.at[block, k],
            device_id=(leaf, to),
            device_id_type=MESH,
        )

    def tile_copy(block, n):
        return pltpu.make_async_remote_copy(
            src_ref=made.at[block, pl.ds(n * tall, tall)],
            dst_ref=taken.at[block, pl.ds(n * tall, tall)],
            send_sem=tile_send.at[block, n],
            recv_sem=tile_recv.at[block, n],
            device_id=(leaf, mate * 2 + c),
            device_id_type=MESH,
        )

    def both(block, n):
        at = pl.ds(n * tall, tall)
        result = lax.dot_general(
            held[block, at], pair[...], (((1,), (1,)), ((), ())),
            preferred_element_type=jnp.float32,
        )
        made[block, at] = result[:, size:]
        tile_copy(block, n).start()
        schur[block, at] = front[block, at] - result[:, :size]

    far_inner, far_outer = across, nz - 1 - mate

    def inner_start():
        for k in range(chunks):
            pass_on(ACROSS, panel, f, k).start()
        for k in range(chunks):
            pass_on(SIDE, panel, f, k).start()
        for k in range(chunks):
            pass_on(MATE, panel, f, k).start()
        product(panel, f)
        for k in range(chunks):
            arrived(side, k)
        product(held.at[side], side)
        near, far = mate * 2 + c, far_inner * 2 + c
        for k in range(chunks):
            arrived(near, k)
            pass_on(ACROSS, held.at[near], near, k).start()
            pass_on(SIDE, held.at[near], near, k).start()
            arrived(far, k)
            pass_on(SIDE, held.at[far], far, k).start()
        pair[pl.ds(size, size)] = held[near]
        for n in range(pieces):
            both(far, n)
        far = far_inner * 2 + 1 - c
        for k in range(chunks):
            arrived(far, k)
        for n in range(pieces):
            both(far, n)
        product(held.at[near], near)
        near = mate * 2 + 1 - c
        for k in range(chunks):
            arrived(near, k)
        product(held.at[near], near)
        far, other = far_outer * 2 + c, far_outer * 2 + 1 - c
        for n in range(pieces):
            part = range(n * chunks // pieces, (n + 1) * chunks // pieces)
            for k in part:
                arrived(far, k)
                pass_on(SIDE, held.at[far], far, k).start()
            both(far, n)
            for k in part:
                arrived(other, k)
            both(other, n)

    def outer_start():
        for k in range(chunks):
            pass_on(MATE, panel, f, k).start()
        for k in range(chunks):
            pass_on(SIDE, panel, f, k).start()
        product(panel, f)
        for k in range(chunks):
            arrived(side, k)
        product(held.at[side], side)
        near, other = mate * 2 + c, mate * 2 + 1 - c
        for k in range(chunks):
            arrived(near, k)
            pass_on(SIDE, held.at[near], near, k).start()
        product(held.at[near], near)
        for k in range(chunks):
            arrived(other, k)
        product(held.at[other], other)
        for there in (far_outer, far_inner):
            for n in range(pieces):
                at = pl.ds(n * tall, tall)
                for b in (there * 2 + c, there * 2 + 1 - c):
                    tile_copy(b, n).wait_recv()
                    schur[b, at] = front[b, at] - taken[b, at]

    def inner_settle():
        for k in range(chunks):
            for way in (ACROSS, MATE, SIDE):
                pass_on(way, panel, f, k).wait_send()
            for way in (ACROSS, SIDE):
                pass_on(way, panel, mate * 2 + c, k).wait_send()
            pass_on(SIDE, panel, far_inner * 2 + c, k).wait_send()
            pass_on(SIDE, panel, far_outer * 2 + c, k).wait_send()
        for there in (far_outer, far_inner):
            for n in range(pieces):
                for b in (there * 2, there * 2 + 1):
                    tile_copy(b, n).wait_send()

    def outer_settle():
        for k in range(chunks):
            pass_on(MATE, panel, f, k).wait_send()
            pass_on(SIDE, panel, f, k).wait_send()
            pass_on(SIDE, panel, mate * 2 + c, k).wait_send()

    loads[2].wait()

    def find(d):
        row, present = jnp.int32(0), jnp.int32(0)
        for i in range(blocks):
            hit = targets[0, i] == d
            row = jnp.where(hit, i, row)
            present = jnp.where(hit, 1, present)
        return row, present

    chosen = [find((leaf + j) % n_leaf) for j in range(n_leaf)]

    halves = nz == 4
    if halves:
        pl.when(inner)(inner_start)
        pl.when(jnp.logical_not(inner))(outer_start)
    else:
        relay()


    def pick(j):
        row, present = chosen[j]
        tile = schur[row]
        return jnp.where(present > 0, tile, jnp.zeros_like(tile))

    def leaf_copy(j):
        return pltpu.make_async_remote_copy(
            src_ref=message.at[j],
            dst_ref=received.at[leaf],
            send_sem=leaf_send.at[j],
            recv_sem=leaf_recv.at[leaf],
            device_id=((leaf + j) % n_leaf, f),
            device_id_type=MESH,
        )

    for j in range(1, n_leaf):
        message[j] = pick(j)
        leaf_copy(j).start()
    message[0] = pick(0)
    keep = pltpu.make_async_copy(message.at[0], received.at[leaf], leaf_recv.at[leaf])
    keep.start()

    if halves:
        pl.when(inner)(inner_settle)
        pl.when(jnp.logical_not(inner))(outer_settle)
    else:
        relay_settle()
    for j in range(1, n_leaf):
        g = (leaf + n_leaf - j) % n_leaf
        pltpu.make_async_remote_copy(
            src_ref=message.at[j],
            dst_ref=received.at[g],
            send_sem=leaf_send.at[j],
            recv_sem=leaf_recv.at[g],
            device_id=((leaf + j) % n_leaf, f),
            device_id_type=MESH,
        ).wait_recv()
    keep.wait()
    for j in range(1, n_leaf):
        leaf_copy(j).wait_send()


def extend_add(ancestor, received, extend, out):
    first = pl.program_id(0) * out.shape[0]
    out[...] = ancestor[...]
    for g in range(received.shape[0]):
        slot = extend[0, g] - first

        @pl.when((slot >= 0) & (slot < out.shape[0]))
        def _():
            out[slot] += received[g]


def shards(factored_panel, front_tiles, ancestor_tiles, send_slots, extend_slots):
    n_leaf = lax.axis_size("leaf")
    n_front = lax.axis_size("front")
    nz = n_front // 2
    chunks = max(1, 8 // nz)
    blocks, tile_size = front_tiles.shape[0], front_tiles.shape[1]
    rows, width = factored_panel.shape
    hbm = pl.BlockSpec(memory_space=pltpu.HBM)
    received = pl.pallas_call(
        functools.partial(kernel, nz, n_leaf, chunks),
        out_shape=jax.ShapeDtypeStruct((n_leaf, tile_size, tile_size), jnp.float32),
        in_specs=[hbm] * 3,
        out_specs=hbm,
        scratch_shapes=[
            pltpu.VMEM((2 * rows, width), jnp.bfloat16),
            pltpu.VMEM(front_tiles.shape, jnp.float32),
            pltpu.SMEM(send_slots.shape, jnp.int32),
            pltpu.VMEM((n_front, rows, width), jnp.bfloat16),
            pltpu.VMEM((blocks, tile_size, tile_size), jnp.float32),
            pltpu.VMEM((blocks, tile_size, tile_size), jnp.float32),
            pltpu.VMEM((blocks, tile_size, tile_size), jnp.float32),
            pltpu.VMEM((n_leaf, tile_size, tile_size), jnp.float32),
            pltpu.SemaphoreType.DMA((3,)),
            pltpu.SemaphoreType.DMA((3, n_front, chunks)),
            pltpu.SemaphoreType.DMA((n_front, chunks)),
            pltpu.SemaphoreType.DMA((blocks, 2)),
            pltpu.SemaphoreType.DMA((blocks, 2)),
            pltpu.SemaphoreType.DMA((n_leaf,)),
            pltpu.SemaphoreType.DMA((n_leaf,)),
        ],
        compiler_params=pltpu.CompilerParams(
            collective_id=0, has_side_effects=True, vmem_limit_bytes=63 * 1024 * 1024
        ),
        cost_estimate=pl.CostEstimate(
            flops=2 * blocks * tile_size * rows * width,
            bytes_accessed=2 * n_front * rows * width,
            transcendentals=0,
        ),
    )(factored_panel, front_tiles, send_slots)
    held = ancestor_tiles.shape[0]
    group = held // 2 if held % 2 == 0 else held
    part = pl.BlockSpec((group, tile_size, tile_size), lambda n: (n, 0, 0))
    return pl.pallas_call(
        extend_add,
        grid=(held // group,),
        out_shape=jax.ShapeDtypeStruct(ancestor_tiles.shape, jnp.float32),
        in_specs=[
            part,
            pl.BlockSpec((n_leaf, tile_size, tile_size), lambda n: (0, 0, 0)),
            pl.BlockSpec(memory_space=pltpu.SMEM),
        ],
        out_specs=part,
    )(ancestor_tiles, received, extend_slots)


def solution(mesh):
    placed = (
        P(("leaf", "front"), None),
        P(("leaf", "front"), None, None),
        P(("leaf", "front"), None, None),
        P(("leaf", "front"), None),
        P(("leaf", "front"), None),
    )
    return jax.shard_map(
        shards,
        mesh=mesh,
        in_specs=placed,
        out_specs=P(("leaf", "front"), None, None),
        check_vma=False,
    )
```
